32 devices in a mesh: mp: 4 (over z), trow: 4 (over x, core), tcol: 2 (over y).
Axes of the slice: x: 2, y: 2, z: 4, core: 2. Of those that a mesh axis runs over, the one named last changes fastest.
Arguments:
- gram: float32 [4, 4096, 4096], P('mp', 'trow', 'tcol'), as said below
- rhs: float32 [256, 4096], P(('mp', 'tcol'), 'trow'), may hold values from -6 to 6
- guess: float32 [256, 4096], P(('mp', 'tcol'), 'trow'), may hold values from -6 to 6
Outputs:
- merged: float32 [256, 4096], P(('mp', 'tcol'), 'trow')
- residual: float32 [256, 4096], P(('mp', 'tcol'), 'trow')
The draws below stay inside these ranges and needn't reach their ends.
Inputs may be any that keep to these rules, and one draw needn't show every extreme that they name: gram holds 4 symmetric positive definite matrices, one per model.
All inputs are finite; a program needn't handle non-finite values.
Results may differ from the reference program's by a relative error of at most 0.0003.
Values sent between devices are 32-bit elements; how exact they have to be, the bound alone decides.
A program may use at most 64 MiB of HBM per device.

```python
import math
import jax
import jax.numpy as jnp
from jax import lax

D = 4096
COLS = 256
ITERS = 2
MODELS = 4


def draw_gram(key, part):
    first, second, third, fourth = jax.random.split(key, 4)
    position = jnp.arange(D, dtype=jnp.float32)
    trend = 1.0 + 2.0 * position / (D - 1)
    lower = -1.0
    lowest = math.log(0.32)
    own_entries = jax.random.uniform(first, (MODELS, D, D), jnp.float32, lower, 1.0)
    shared_entries = jax.random.uniform(fourth, (D, D), jnp.float32, lower, 1.0)
    raw_entries = 0.6 * shared_entries[None, :, :] + 0.8 * own_entries
    symmetric = 0.5 * (raw_entries + jnp.swapaxes(raw_entries, 1, 2))
    common = jnp.exp(jax.random.uniform(second, (D,), jnp.float32, lowest, 0.0)) * trend
    factor = jnp.exp(jax.random.uniform(third, (MODELS, D), jnp.float32, math.log(0.5), math.log(2.0)))
    scaling = jnp.sqrt(common[None, :] * factor / MODELS)
    diagonal_mask = jnp.arange(D)[:, None] == jnp.arange(D)[None, :]
    inner = jnp.where(diagonal_mask[None, :, :], 1.0, 0.8 / math.sqrt(D) * symmetric)
    return scaling[:, :, None] * scaling[:, None, :] * inner


def block_levels(rng, extent, pieces, least, top_value):
    level = 1.0
    for dim, shards_of in pieces:
        heights = jax.random.uniform(jax.random.fold_in(jax.random.fold_in(rng, 6), dim), (shards_of,), jnp.float32, least / len(pieces), top_value / len(pieces))
        level = level * jnp.repeat(jnp.exp(heights), extent[dim] // shards_of).reshape((-1,) + (1,) * (len(extent) - 1 - dim))
    return level


def centred(rng, shape, scale, reach, pieces=(), held_as=jnp.bfloat16):
    array = jax.random.normal(rng, shape, jnp.float32) * scale
    if len(pieces) > 0:
        array = block_levels(rng, shape, pieces, -0.22, 0.18) * array
    return jnp.clip(array, min=-reach, max=reach).astype(held_as)


def setup_inputs(seed: int = 0) -> dict:
    key_list = jax.random.split(jax.random.key(seed), 4)
    gram = draw_gram(jax.random.fold_in(key_list[3], 71), 0)
    rhs = centred(key_list[1], (COLS, D), 1.0, 6.0, ((0, 8), (1, 4)), jnp.float32)
    guess = centred(key_list[2], (COLS, D), 1.0, 6.0, ((0, 8), (1, 4)), jnp.float32)
    return {"gram": gram, "rhs": rhs, "guess": guess}


def reference(gram, rhs, guess):
    total = jnp.sum(gram, axis=0)

    def apply_total(vector):
        return lax.dot_general(vector, total, (((1,), (1,)), ((), ())), precision=lax.Precision.HIGHEST, preferred_element_type=jnp.float32)

    merged = guess
    residual = rhs - apply_total(guess)
    direction = residual
    norm_now = jnp.sum(residual * residual, axis=1)
    for step in range(ITERS):
        image = apply_total(direction)
        alpha = norm_now / jnp.sum(direction * image, axis=1)
        merged = merged + alpha[:, None] * direction
        residual = residual - alpha[:, None] * image
        norm_next = jnp.sum(residual * residual, axis=1)
        direction = residual + (norm_next / norm_now)[:, None] * direction
        norm_now = norm_next
    return merged, residual
```

```python
import functools

import jax
import jax.numpy as jnp
from jax import lax
from jax.experimental import pallas as pl
from jax.experimental.pallas import tpu as pltpu
from jax.sharding import PartitionSpec as P

ITERS = 2
APPS = ITERS + 1
TILE = 256
MESH = pl.DeviceIdType.MESH
NT = (((1,), (1,)), ((), ()))


def swap_bits(index, bits):
    weight = 1
    out = index
    while weight <= bits:
        if (bits // weight) % 2:
            out = out + weight - 2 * weight * ((index // weight) % 2)
        weight *= 2
    return out


def kernel(Z, T, C, gram_ref, rhs_ref, guess_ref, merged_ref, residual_ref,
           stage, g_hi, g_lo, vec, own, full, prod, from_y, summed, from_z, dots, dirn, image,
           stage_sem, g1_s, g1_r, g2_s, g2_r, g3_s, g3_r, r1_s, r1_r, r2_s, r2_r, d_s, d_r):
    H = T // C
    rows, feats = guess_ref.shape
    tiles = feats // TILE
    cols = Z * C * rows
    z, t, y = lax.axis_index("mp"), lax.axis_index("trow"), lax.axis_index("tcol")
    x, c = t // H, t % H
    diagonal = x == y

    def gram_copy(n):
        return pltpu.make_async_copy(
            gram_ref.at[0, pl.ds(n * TILE, TILE)], stage.at[n], stage_sem.at[n])

    for n in range(tiles):
        gram_copy(n).start()

    def remote(src, dst, s_sem, r_sem, mp=None, trow=None, tcol=None):
        return pltpu.make_async_remote_copy(
            src_ref=src, dst_ref=dst, send_sem=s_sem, recv_sem=r_sem,
            device_id=(z if mp is None else mp, t if trow is None else trow,
                       y if tcol is None else tcol),
            device_id_type=MESH)

    barrier = pltpu.get_barrier_semaphore()
    for d in range(1, Z):
        pl.semaphore_signal(barrier, inc=1, device_id=(swap_bits(z, d), t, y), device_id_type=MESH)
    for e in range(1, T * C):
        place = (t * C + y + e) % (T * C)
        pl.semaphore_signal(barrier, inc=1, device_id=(z, place // C, place % C), device_id_type=MESH)
    pl.semaphore_wait(barrier, Z - 1 + T * C - 1)

    sends = []

    def g1(a, d):
        return remote(own.at[a, z], own.at[a, z], g1_s.at[a, d], g1_r.at[a, d], mp=swap_bits(z, d))

    def g1_in(a, d):
        zi = swap_bits(z, d)
        return remote(own.at[a, zi], own.at[a, zi], g1_s.at[a, d], g1_r.at[a, d], mp=zi)

    def g2(a, d, xp):
        zi = swap_bits(z, d)
        return remote(own.at[a, zi], full.at[a, c, zi, y], g2_s.at[a, d, xp], g2_r.at[a, d, y],
                      trow=xp * H + c, tcol=x)

    def g2_in(a, d, yp):
        zi = swap_bits(z, d)
        return remote(own.at[a, zi], full.at[a, c, zi, yp], g2_s.at[a, d, yp], g2_r.at[a, d, yp],
                      trow=y * H + c, tcol=yp)

    def g3(a, d, yp, h):
        zi = swap_bits(z, d)
        block = full.at[a, c, zi, yp]
        return remote(block, block, g3_s.at[a, d, yp, h], g3_r.at[a, d, yp, h],
                      trow=x * H + (c + h) % H)

    def g3_in(a, d, yp, h):
        zi = swap_bits(z, d)
        far = (c + H - h) % H
        block = full.at[a, far, zi, yp]
        return remote(block, block, g3_s.at[a, d, yp, h], g3_r.at[a, d, yp, h], trow=x * H + far)

    def push_plane(a, d):
        for xp in range(C):
            away = jnp.logical_not(jnp.logical_and(diagonal, x == xp))

            @pl.when(away)
            def _():
                g2(a, d, xp).start()

    def split_block(a, half, zi, yp):
        value = full[a, half, zi, yp]
        high = value.astype(jnp.bfloat16)
        low = (value - high.astype(jnp.float32)).astype(jnp.bfloat16)
        at = pl.multiple_of((zi * C + yp) * rows, rows)
        lanes = pl.ds(pl.multiple_of(half * feats, feats), feats)
        vec[pl.ds(at, rows), lanes] = high
        vec[pl.ds(cols + at, rows), lanes] = low

    def land_plane(a, d):
        zi = swap_bits(z, d)
        for yp in range(C):
            here = jnp.logical_and(diagonal, y == yp)

            @pl.when(here)
            def _():
                full[a, c, zi, yp] = own[a, zi]

            @pl.when(jnp.logical_not(here))
            def _():
                g2_in(a, d, yp).wait_recv()

            for h in range(1, H):
                g3(a, d, yp, h).start()
            split_block(a, c, zi, yp)

    def land_core(a, d):
        zi = swap_bits(z, d)
        for yp in range(C):
            for h in range(1, H):
                g3_in(a, d, yp, h).wait_recv()
                split_block(a, (c + H - h) % H, zi, yp)

    def start_gather(a):
        for d in range(Z - 1, 0, -1):
            g1(a, d).start()
        push_plane(a, 0)

    def finish_gather(a):
        for d in range(Z + 1):
            if d + 1 < Z:
                g1_in(a, d + 1).wait_recv()
                push_plane(a, d + 1)
            if d < Z:
                land_plane(a, d)
            if d >= 1:
                land_core(a, d - 1)

    def r1(a, n, dy):
        yp = (y + dy) % C
        return remote(prod.at[a, n, yp], from_y.at[a, n, dy], r1_s.at[a, n, dy], r1_r.at[a, n, dy], tcol=yp)

    def r2(a, n, d):
        zi = swap_bits(z, d)
        return remote(summed.at[a, n, zi], from_z.at[a, n, d], r2_s.at[a, n, d], r2_r.at[a, n, d], mp=zi)

    def multiply(a):
        @pl.loop(0, tiles)
        def _(n):
            at = pl.ds(pl.multiple_of(n * TILE, TILE), TILE)
            main = lax.dot_general(vec[...], g_hi[at, :], NT, preferred_element_type=jnp.float32)
            rest = lax.dot_general(vec[0:cols, :], g_lo[at, :], NT, preferred_element_type=jnp.float32)
            total = main[0:cols] + (main[cols:2 * cols] + rest)
            for zi in range(Z):
                for yp in range(C):
                    row = (zi * C + yp) * rows
                    prod[a, n, yp, zi] = total[row:row + rows]
            for dy in range(1, C):
                r1(a, n, dy).start()

    def scatter(a):
        for n in range(tiles):
            for dy in range(1, C):
                r1(a, n, dy).wait_recv()
            total = prod[a, n, y]
            for dy in range(1, C):
                total = total + from_y[a, n, dy]
            summed[a, n] = total
            for d in range(Z - 1, 0, -1):
                r2(a, n, d).start()
        for n in range(tiles):
            part = summed[a, n, z]
            for d in range(1, Z):
                r2(a, n, d).wait_recv()
                part = part + from_z[a, n, d]
            image[:, n * TILE:(n + 1) * TILE] = part

    def dot_copy(k, e):
        return remote(dots.at[k, t], dots.at[k, t], d_s.at[k, e], d_r.at[k, e], trow=(t + e) % T)

    def dot_in(k, e):
        far = (t + T - e) % T
        return remote(dots.at[k, far], dots.at[k, far], d_s.at[k, e], d_r.at[k, e], trow=far)

    def dot_start(k, value):
        dots[k, t] = jnp.broadcast_to(jnp.sum(value, axis=1, keepdims=True), (rows, 128))
        for e in range(1, T):
            dot_copy(k, e).start()

    def dot_finish(k):
        for e in range(1, T):
            dot_in(k, e).wait_recv()
        total = dots[k, 0]
        for e in range(1, T):
            total = total + dots[k, e]
        return total[:, 0:1]

    own[0, z] = guess_ref[...]
    start_gather(0)
    for n in range(tiles):
        gram_copy(n).wait()

        @pl.loop(0, TILE // 32)
        def _(i):
            value = stage[n, pl.ds(pl.multiple_of(i * 32, 32), 32)]
            high = value.astype(jnp.bfloat16)
            at = pl.ds(pl.multiple_of(n * TILE + i * 32, 32), 32)
            g_hi[at, :] = high
            g_lo[at, :] = (value - high.astype(jnp.float32)).astype(jnp.bfloat16)

    finish_gather(0)
    multiply(0)
    scatter(0)
    residual = rhs_ref[...] - image[...]
    residual_ref[...] = residual
    own[1, z] = residual
    dirn[...] = residual
    merged_ref[...] = guess_ref[...]
    start_gather(1)
    dot_start(0, residual * residual)
    norm_now = None
    for step in range(ITERS):
        a = step + 1
        finish_gather(a)
        multiply(a)
        scatter(a)
        dot_start(2 * step + 1, dirn[...] * image[...])
        if step == 0:
            norm_now = dot_finish(0)
        alpha = norm_now / dot_finish(2 * step + 1)
        residual = residual_ref[...] - alpha * image[...]
        residual_ref[...] = residual
        if step + 1 < ITERS:
            dot_start(2 * step + 2, residual * residual)
            merged_ref[...] = merged_ref[...] + alpha * dirn[...]
            norm_next = dot_finish(2 * step + 2)
            direction = residual + (norm_next / norm_now) * dirn[...]
            dirn[...] = direction
            own[a + 1, z] = direction
            start_gather(a + 1)
            norm_now = norm_next
        else:
            merged_ref[...] = merged_ref[...] + alpha * dirn[...]

    for a in range(APPS):
        for d in range(1, Z):
            g1(a, d).wait_send()
        for d in range(Z):
            for xp in range(C):
                away = jnp.logical_not(jnp.logical_and(diagonal, x == xp))

                @pl.when(away)
                def _():
                    g2(a, d, xp).wait_send()

                for h in range(1, H):
                    g3(a, d, xp, h).wait_send()
        for n in range(tiles):
            for dy in range(1, C):
                r1(a, n, dy).wait_send()
            for d in range(1, Z):
                r2(a, n, d).wait_send()
    for k in range(2 * ITERS):
        for e in range(1, T):
            dot_copy(k, e).wait_send()


def kernel_shards(Z, T, C, gram, rhs, guess):
    H = T // C
    rows, feats = guess.shape
    tiles = feats // TILE
    cols = Z * C * rows
    f32, bf16 = jnp.float32, jnp.bfloat16
    dma = pltpu.SemaphoreType.DMA
    vmem = pl.BlockSpec(memory_space=pltpu.VMEM)
    shape = jax.ShapeDtypeStruct(guess.shape, f32)
    scratch = [
        pltpu.VMEM((tiles, TILE, H * feats), f32),
        pltpu.VMEM((feats, H * feats), bf16),
        pltpu.VMEM((feats, H * feats), bf16),
        pltpu.VMEM((2 * cols, H * feats), bf16),
        pltpu.VMEM((APPS, Z, rows, feats), f32),
        pltpu.VMEM((APPS, H, Z, C, rows, feats), f32),
        pltpu.VMEM((APPS, tiles, C, Z, rows, TILE), f32),
        pltpu.VMEM((APPS, tiles, C, Z, rows, TILE), f32),
        pltpu.VMEM((APPS, tiles, Z, rows, TILE), f32),
        pltpu.VMEM((APPS, tiles, Z, rows, TILE), f32),
        pltpu.VMEM((2 * ITERS, T, rows, 128), f32),
        pltpu.VMEM((rows, feats), f32),
        pltpu.VMEM((rows, feats), f32),
        dma((tiles,)),
        dma((APPS, Z)), dma((APPS, Z)),
        dma((APPS, Z, C)), dma((APPS, Z, C)),
        dma((APPS, Z, C, H)), dma((APPS, Z, C, H)),
        dma((APPS, tiles, C)), dma((APPS, tiles, C)),
        dma((APPS, tiles, Z)), dma((APPS, tiles, Z)),
        dma((2 * ITERS, T)), dma((2 * ITERS, T)),
    ]
    return pl.pallas_call(
        functools.partial(kernel, Z, T, C),
        out_shape=(shape, shape),
        in_specs=[pl.BlockSpec(memory_space=pl.ANY), vmem, vmem],
        out_specs=(vmem, vmem),
        scratch_shapes=scratch,
        cost_estimate=pl.CostEstimate(
            flops=APPS * 6 * cols * feats * H * feats,
            bytes_accessed=gram.size * 4,
            transcendentals=0),
        compiler_params=pltpu.CompilerParams(
            collective_id=0, has_side_effects=True, vmem_limit_bytes=56 * 1024 * 1024),
    )(gram, rhs, guess)


def general_shards(gram, rhs, guess):
    gram_tile = gram[0]
    block_cols = gram_tile.shape[1]

    def apply_total(vector):
        columns = lax.all_gather(vector, ("mp", "tcol"), axis=0, tiled=True)
        gathered = lax.all_gather(columns, "trow", axis=1, tiled=True)
        block = lax.dynamic_slice_in_dim(
            gathered, lax.axis_index("tcol") * block_cols, block_cols, 1)
        terms = lax.dot_general(block, gram_tile, NT, precision=lax.Precision.HIGHEST,
                                preferred_element_type=jnp.float32)
        return lax.psum_scatter(terms, ("mp", "tcol"), scatter_dimension=0, tiled=True)

    def squares(values):
        return lax.psum(jnp.sum(values * values, axis=1), "trow")

    merged = guess
    residual = rhs - apply_total(guess)
    direction = residual
    norm_now = squares(residual)
    for step in range(ITERS):
        image = apply_total(direction)
        curve = lax.psum(jnp.sum(direction * image, axis=1), "trow")
        alpha = norm_now / curve
        merged = merged + alpha[:, None] * direction
        residual = residual - alpha[:, None] * image
        if step + 1 < ITERS:
            norm_next = squares(residual)
            direction = residual + (norm_next / norm_now)[:, None] * direction
            norm_now = norm_next
    return (merged, residual)


def solution(mesh):
    Z, T, C = mesh.shape["mp"], mesh.shape["trow"], mesh.shape["tcol"]

    def shards(gram, rhs, guess):
        rows, feats = guess.shape
        fits = T % C == 0 and Z & (Z - 1) == 0 and rows % 16 == 0 and feats % TILE == 0
        fits = fits and Z * C * rows * feats <= 256 * 1024 and gram.shape[0] == 1
        if fits:
            return kernel_shards(Z, T, C, gram, rhs, guess)
        return general_shards(gram, rhs, guess)

    in_specs = (P("mp", "trow", "tcol"), P(("mp", "tcol"), "trow"), P(("mp", "tcol"), "trow"))
    out_specs = (P(("mp", "tcol"), "trow"), P(("mp", "tcol"), "trow"))
    return jax.shard_map(shards, mesh=mesh, in_specs=in_specs, out_specs=out_specs, check_vma=False)
```

```python
import functools

import jax
import jax.numpy as jnp
from jax import lax
from jax.experimental import pallas as pl
from jax.experimental.pallas import tpu as pltpu
from jax.sharding import PartitionSpec as P

ITERS = 2
APPS = ITERS + 1
TILE = 256
MESH = pl.DeviceIdType.MESH
NT = (((1,), (1,)), ((), ()))


def swap_bits(index, bits):
    weight = 1
    out = index
    while weight <= bits:
        if (bits // weight) % 2:
            out = out + weight - 2 * weight * ((index // weight) % 2)
        weight *= 2
    return out


def kernel(Z, T, C, gram_ref, rhs_ref, guess_ref, merged_ref, residual_ref,
           stage, g_hi, g_lo, vec, own, full, prod, from_y, summed, from_z, dots, dirn, image,
           stage_sem, g1_s, g1_r, g2_s, g2_r, g3_s, g3_r, r1_s, r1_r, r2_s, r2_r, d_s, d_r):
    H = T // C
    rows, feats = guess_ref.shape
    tiles = feats // TILE
    cols = Z * C * rows
    z, t, y = lax.axis_index("mp"), lax.axis_index("trow"), lax.axis_index("tcol")
    x, c = t // H, t % H
    diagonal = x == y

    def gram_copy(n):
        return pltpu.make_async_copy(
            gram_ref.at[0, pl.ds(n * TILE, TILE)], stage.at[n], stage_sem.at[n])

    for n in range(tiles):
        gram_copy(n).start()

    def remote(src, dst, s_sem, r_sem, mp=None, trow=None, tcol=None):
        return pltpu.make_async_remote_copy(
            src_ref=src, dst_ref=dst, send_sem=s_sem, recv_sem=r_sem,
            device_id=(z if mp is None else mp, t if trow is None else trow,
                       y if tcol is None else tcol),
            device_id_type=MESH)

    barrier = pltpu.get_barrier_semaphore()
    for d in range(1, Z):
        pl.semaphore_signal(barrier, inc=1, device_id=(swap_bits(z, d), t, y), device_id_type=MESH)
    for e in range(1, T * C):
        place = (t * C + y + e) % (T * C)
        pl.semaphore_signal(barrier, inc=1, device_id=(z, place // C, place % C), device_id_type=MESH)
    pl.semaphore_wait(barrier, Z - 1 + T * C - 1)

    sends = []

    steps = [(0, 0)] + [(k, side) for k in range(1, Z) for side in (-1, 1)]

    def block_of(step):
        return z + step[0] * step[1]

    def exists(step):
        if step[0] == 0:
            return True
        return z >= step[0] if step[1] < 0 else z + step[0] < Z

    def when(condition, act):
        if condition is True:
            act()
        else:
            pl.when(condition)(act)

    def g1(a, zi, way):
        block = own.at[a, zi]
        return remote(block, block, g1_s.at[a, (way + 1) // 2, zi], g1_r.at[a, zi], mp=z + way)

    def pass_on(a, step, act):
        zi = block_of(step)
        for way in (-1, 1):
            if step[0] == 0 or step[1] == -way:
                more = z > 0 if way < 0 else z < Z - 1
                if step[0]:
                    more = jnp.logical_and(more, exists(step))
                when(more, lambda way=way: act(g1(a, zi, way)))

    def g2(a, d, xp):
        zi = block_of(d)
        return remote(own.at[a, zi], full.at[a, c, zi, y], g2_s.at[a, zi, xp], g2_r.at[a, zi, y],
                      trow=xp * H + c, tcol=x)

    def g2_in(a, d, yp):
        zi = block_of(d)
        return remote(own.at[a, zi], full.at[a, c, zi, yp], g2_s.at[a, zi, yp], g2_r.at[a, zi, yp],
                      trow=y * H + c, tcol=yp)

    def g3(a, d, yp, h):
        zi = block_of(d)
        block = full.at[a, c, zi, yp]
        return remote(block, block, g3_s.at[a, zi, yp, h], g3_r.at[a, zi, yp, h],
                      trow=x * H + (c + h) % H)

    def g3_in(a, d, yp, h):
        zi = block_of(d)
        far = (c + H - h) % H
        block = full.at[a, far, zi, yp]
        return remote(block, block, g3_s.at[a, zi, yp, h], g3_r.at[a, zi, yp, h], trow=x * H + far)

    def push_plane(a, d):
        for xp in range(C):
            away = jnp.logical_not(jnp.logical_and(diagonal, x == xp))

            @pl.when(away)
            def _():
                g2(a, d, xp).start()

    def split_block(a, half, zi, yp):
        value = full[a, half, zi, yp]
        high = value.astype(jnp.bfloat16)
        low = (value - high.astype(jnp.float32)).astype(jnp.bfloat16)
        at = pl.multiple_of((zi * C + yp) * rows, rows)
        lanes = pl.ds(pl.multiple_of(half * feats, feats), feats)
        vec[pl.ds(at, rows), lanes] = high
        vec[pl.ds(cols + at, rows), lanes] = low

    def land_plane(a, d):
        zi = block_of(d)
        for yp in range(C):
            here = jnp.logical_and(diagonal, y == yp)

            @pl.when(here)
            def _():
                full[a, c, zi, yp] = own[a, zi]

            @pl.when(jnp.logical_not(here))
            def _():
                g2_in(a, d, yp).wait_recv()

            for h in range(1, H):
                g3(a, d, yp, h).start()
            split_block(a, c, zi, yp)

    def land_core(a, d):
        zi = block_of(d)
        for yp in range(C):
            for h in range(1, H):
                g3_in(a, d, yp, h).wait_recv()
                split_block(a, (c + H - h) % H, zi, yp)

    def start_gather(a):
        pass_on(a, steps[0], lambda copy: copy.start())
        push_plane(a, steps[0])

    def arrive(a, step):
        zi = block_of(step)
        g1(a, zi, step[1]).wait_recv()
        pass_on(a, step, lambda copy: copy.start())
        push_plane(a, step)

    def finish_gather(a):
        count = len(steps)
        for i in range(count + 2):
            if 1 <= i < count:
                when(exists(steps[i]), lambda i=i: arrive(a, steps[i]))
            if 2 <= i + 1 <= count + 1 and 0 <= i - 1 < count:
                when(exists(steps[i - 1]), lambda i=i: land_plane(a, steps[i - 1]))
            if 0 <= i - 2 < count:
                when(exists(steps[i - 2]), lambda i=i: land_core(a, steps[i - 2]))

    def r1(a, n, dy):
        yp = (y + dy) % C
        return remote(prod.at[a, n, yp], from_y.at[a, n, dy], r1_s.at[a, n, dy], r1_r.at[a, n, dy], tcol=yp)

    def r2(a, n, d):
        zi = swap_bits(z, d)
        return remote(summed.at[a, n, zi], from_z.at[a, n, d], r2_s.at[a, n, d], r2_r.at[a, n, d], mp=zi)

    def multiply(a):
        @pl.loop(0, tiles)
        def _(n):
            at = pl.ds(pl.multiple_of(n * TILE, TILE), TILE)
            main = lax.dot_general(vec[...], g_hi[at, :], NT, preferred_element_type=jnp.float32)
            rest = lax.dot_general(vec[0:cols, :], g_lo[at, :], NT, preferred_element_type=jnp.float32)
            total = main[0:cols] + (main[cols:2 * cols] + rest)
            for zi in range(Z):
                for yp in range(C):
                    row = (zi * C + yp) * rows
                    prod[a, n, yp, zi] = total[row:row + rows]

            @pl.when(n < 2)
            def _():
                for dy in range(1, C):
                    r1(a, n, dy).start()

    def scatter(a):
        for n in range(tiles):
            for dy in range(1, C):
                r1(a, n, dy).wait_recv()
                r1(a, n, dy).wait_send()
                if n + 2 < tiles:
                    r1(a, n + 2, dy).start()
            total = prod[a, n, y]
            for dy in range(1, C):
                total = total + from_y[a, n, dy]
            summed[a, n] = total
            for d in range(Z - 1, 0, -1):
                r2(a, n, d).start()
        for n in range(tiles):
            part = summed[a, n, z]
            for d in range(1, Z):
                r2(a, n, d).wait_recv()
                part = part + from_z[a, n, d]
            image[:, n * TILE:(n + 1) * TILE] = part

    def dot_copy(k, e):
        return remote(dots.at[k, t], dots.at[k, t], d_s.at[k, e], d_r.at[k, e], trow=(t + e) % T)

    def dot_in(k, e):
        far = (t + T - e) % T
        return remote(dots.at[k, far], dots.at[k, far], d_s.at[k, e], d_r.at[k, e], trow=far)

    def dot_start(k, value):
        dots[k, t] = jnp.broadcast_to(jnp.sum(value, axis=1, keepdims=True), (rows, 128))
        for e in range(1, T):
            dot_copy(k, e).start()

    def dot_finish(k):
        for e in range(1, T):
            dot_in(k, e).wait_recv()
        total = dots[k, 0]
        for e in range(1, T):
            total = total + dots[k, e]
        return total[:, 0:1]

    own[0, z] = guess_ref[...]
    start_gather(0)
    for n in range(tiles):
        gram_copy(n).wait()

        @pl.loop(0, TILE // 32)
        def _(i):
            value = stage[n, pl.ds(pl.multiple_of(i * 32, 32), 32)]
            high = value.astype(jnp.bfloat16)
            at = pl.ds(pl.multiple_of(n * TILE + i * 32, 32), 32)
            g_hi[at, :] = high
            g_lo[at, :] = (value - high.astype(jnp.float32)).astype(jnp.bfloat16)

    finish_gather(0)
    multiply(0)
    scatter(0)
    residual = rhs_ref[...] - image[...]
    residual_ref[...] = residual
    own[1, z] = residual
    dirn[...] = residual
    merged_ref[...] = guess_ref[...]
    start_gather(1)
    dot_start(0, residual * residual)
    norm_now = None
    for step in range(ITERS):
        a = step + 1
        finish_gather(a)
        multiply(a)
        scatter(a)
        dot_start(2 * step + 1, dirn[...] * image[...])
        if step == 0:
            norm_now = dot_finish(0)
        alpha = norm_now / dot_finish(2 * step + 1)
        residual = residual_ref[...] - alpha * image[...]
        residual_ref[...] = residual
        if step + 1 < ITERS:
            dot_start(2 * step + 2, residual * residual)
            merged_ref[...] = merged_ref[...] + alpha * dirn[...]
            norm_next = dot_finish(2 * step + 2)
            direction = residual + (norm_next / norm_now) * dirn[...]
            dirn[...] = direction
            own[a + 1, z] = direction
            start_gather(a + 1)
            norm_now = norm_next
        else:
            merged_ref[...] = merged_ref[...] + alpha * dirn[...]

    def end_block(a, step):
        pass_on(a, step, lambda copy: copy.wait_send())
        for xp in range(C):
            away = jnp.logical_not(jnp.logical_and(diagonal, x == xp))

            @pl.when(away)
            def _():
                g2(a, step, xp).wait_send()

            for h in range(1, H):
                g3(a, step, xp, h).wait_send()

    for a in range(APPS):
        for step in steps:
            when(exists(step), lambda: end_block(a, step))
        for n in range(tiles):
            for d in range(1, Z):
                r2(a, n, d).wait_send()
    for k in range(2 * ITERS):
        for e in range(1, T):
            dot_copy(k, e).wait_send()


def kernel_shards(Z, T, C, gram, rhs, guess):
    H = T // C
    rows, feats = guess.shape
    tiles = feats // TILE
    cols = Z * C * rows
    f32, bf16 = jnp.float32, jnp.bfloat16
    dma = pltpu.SemaphoreType.DMA
    vmem = pl.BlockSpec(memory_space=pltpu.VMEM)
    shape = jax.ShapeDtypeStruct(guess.shape, f32)
    scratch = [
        pltpu.VMEM((tiles, TILE, H * feats), f32),
        pltpu.VMEM((feats, H * feats), bf16),
        pltpu.VMEM((feats, H * feats), bf16),
        pltpu.VMEM((2 * cols, H * feats), bf16),
        pltpu.VMEM((APPS, Z, rows, feats), f32),
        pltpu.VMEM((APPS, H, Z, C, rows, feats), f32),
        pltpu.VMEM((APPS, tiles, C, Z, rows, TILE), f32),
        pltpu.VMEM((APPS, tiles, C, Z, rows, TILE), f32),
        pltpu.VMEM((APPS, tiles, Z, rows, TILE), f32),
        pltpu.VMEM((APPS, tiles, Z, rows, TILE), f32),
        pltpu.VMEM((2 * ITERS, T, rows, 128), f32),
        pltpu.VMEM((rows, feats), f32),
        pltpu.VMEM((rows, feats), f32),
        dma((tiles,)),
        dma((APPS, 2, Z)), dma((APPS, Z)),
        dma((APPS, Z, C)), dma((APPS, Z, C)),
        dma((APPS, Z, C, H)), dma((APPS, Z, C, H)),
        dma((APPS, tiles, C)), dma((APPS, tiles, C)),
        dma((APPS, tiles, Z)), dma((APPS, tiles, Z)),
        dma((2 * ITERS, T)), dma((2 * ITERS, T)),
    ]
    return pl.pallas_call(
        functools.partial(kernel, Z, T, C),
        out_shape=(shape, shape),
        in_specs=[pl.BlockSpec(memory_space=pl.ANY), vmem, vmem],
        out_specs=(vmem, vmem),
        scratch_shapes=scratch,
        cost_estimate=pl.CostEstimate(
            flops=APPS * 6 * cols * feats * H * feats,
            bytes_accessed=gram.size * 4,
            transcendentals=0),
        compiler_params=pltpu.CompilerParams(
            collective_id=0, has_side_effects=True, vmem_limit_bytes=56 * 1024 * 1024),
    )(gram, rhs, guess)


def general_shards(gram, rhs, guess):
    gram_tile = gram[0]
    block_cols = gram_tile.shape[1]

    def apply_total(vector):
        columns = lax.all_gather(vector, ("mp", "tcol"), axis=0, tiled=True)
        gathered = lax.all_gather(columns, "trow", axis=1, tiled=True)
        block = lax.dynamic_slice_in_dim(
            gathered, lax.axis_index("tcol") * block_cols, block_cols, 1)
        terms = lax.dot_general(block, gram_tile, NT, precision=lax.Precision.HIGHEST,
                                preferred_element_type=jnp.float32)
        return lax.psum_scatter(terms, ("mp", "tcol"), scatter_dimension=0, tiled=True)

    def squares(values):
        return lax.psum(jnp.sum(values * values, axis=1), "trow")

    merged = guess
    residual = rhs - apply_total(guess)
    direction = residual
    norm_now = squares(residual)
    for step in range(ITERS):
        image = apply_total(direction)
        curve = lax.psum(jnp.sum(direction * image, axis=1), "trow")
        alpha = norm_now / curve
        merged = merged + alpha[:, None] * direction
        residual = residual - alpha[:, None] * image
        if step + 1 < ITERS:
            norm_next = squares(residual)
            direction = residual + (norm_next / norm_now)[:, None] * direction
            norm_now = norm_next
    return (merged, residual)


def solution(mesh):
    Z, T, C = mesh.shape["mp"], mesh.shape["trow"], mesh.shape["tcol"]

    def shards(gram, rhs, guess):
        rows, feats = guess.shape
        fits = T % C == 0 and Z & (Z - 1) == 0 and rows % 16 == 0 and feats % TILE == 0
        fits = fits and Z * C * rows * feats <= 256 * 1024 and gram.shape[0] == 1
        if fits:
            return kernel_shards(Z, T, C, gram, rhs, guess)
        return general_shards(gram, rhs, guess)

    in_specs = (P("mp", "trow", "tcol"), P(("mp", "tcol"), "trow"), P(("mp", "tcol"), "trow"))
    out_specs = (P(("mp", "tcol"), "trow"), P(("mp", "tcol"), "trow"))
    return jax.shard_map(shards, mesh=mesh, in_specs=in_specs, out_specs=out_specs, check_vma=False)
```

```python
import functools

import jax
import jax.numpy as jnp
from jax import lax
from jax.experimental import pallas as pl
from jax.experimental.pallas import tpu as pltpu
from jax.sharding import PartitionSpec as P

ITERS = 2
APPS = ITERS + 1
TILE = 512
GROUPS = 2
MESH = pl.DeviceIdType.MESH
NT = (((1,), (1,)), ((), ()))


def swap_bits(index, bits):
    weight = 1
    out = index
    while weight <= bits:
        if (bits // weight) % 2:
            out = out + weight - 2 * weight * ((index // weight) % 2)
        weight *= 2
    return out


def kernel(Z, T, C, gram_ref, rhs_ref, guess_ref, merged_ref, residual_ref,
           stage, g_hi, g_lo, vec, own, full, prod, from_y, summed, from_z, dots, dirn, image,
           stage_sem, g1_s, g1_r, g2_s, g2_r, g3_s, g3_r, r1_s, r1_r, r2_s, r2_r, d_s, d_r):
    H = T // C
    rows, feats = guess_ref.shape[0] // GROUPS, guess_ref.shape[1]
    tiles = feats // TILE
    cols = Z * C * rows
    z, t, y = lax.axis_index("mp"), lax.axis_index("trow"), lax.axis_index("tcol")
    x, c = t // H, t % H
    diagonal = x == y

    def gram_copy(n):
        return pltpu.make_async_copy(
            gram_ref.at[0, pl.ds(n * TILE, TILE)], stage.at[n], stage_sem.at[n])

    for n in range(tiles):
        gram_copy(n).start()

    def remote(src, dst, s_sem, r_sem, mp=None, trow=None, tcol=None):
        return pltpu.make_async_remote_copy(
            src_ref=src, dst_ref=dst, send_sem=s_sem, recv_sem=r_sem,
            device_id=(z if mp is None else mp, t if trow is None else trow,
                       y if tcol is None else tcol),
            device_id_type=MESH)

    barrier = pltpu.get_barrier_semaphore()
    for d in range(1, Z):
        pl.semaphore_signal(barrier, inc=1, device_id=(swap_bits(z, d), t, y), device_id_type=MESH)
    for e in range(1, T * C):
        place = (t * C + y + e) % (T * C)
        pl.semaphore_signal(barrier, inc=1, device_id=(z, place // C, place % C), device_id_type=MESH)
    pl.semaphore_wait(barrier, Z - 1 + T * C - 1)

    steps = [(0, 0)] + [(k, side) for k in range(1, Z) for side in (-1, 1)]

    def block_of(step):
        return z + step[0] * step[1]

    def exists(step):
        if step[0] == 0:
            return True
        return z >= step[0] if step[1] < 0 else z + step[0] < Z

    def when(condition, act):
        if condition is True:
            act()
        else:
            pl.when(condition)(act)

    def g1(a, zi, way):
        block = own.at[a, zi]
        return remote(block, block, g1_s.at[a, (way + 1) // 2, zi], g1_r.at[a, zi], mp=z + way)

    def pass_on(a, step, act):
        zi = block_of(step)
        for way in (-1, 1):
            if step[0] == 0 or step[1] == -way:
                more = z > 0 if way < 0 else z < Z - 1
                if step[0]:
                    more = jnp.logical_and(more, exists(step))
                when(more, lambda way=way: act(g1(a, zi, way)))

    def g2(a, d, xp):
        zi = block_of(d)
        return remote(own.at[a, zi], full.at[a, c, zi, y], g2_s.at[a, zi, xp], g2_r.at[a, zi, y],
                      trow=xp * H + c, tcol=x)

    def g2_in(a, d, yp):
        zi = block_of(d)
        return remote(own.at[a, zi], full.at[a, c, zi, yp], g2_s.at[a, zi, yp], g2_r.at[a, zi, yp],
                      trow=y * H + c, tcol=yp)

    def g3(a, d, yp, h):
        zi = block_of(d)
        block = full.at[a, c, zi, yp]
        return remote(block, block, g3_s.at[a, zi, yp, h - 1], g3_r.at[a, zi, yp, h - 1],
                      trow=x * H + (c + h) % H)

    def g3_in(a, d, yp, h):
        zi = block_of(d)
        far = (c + H - h) % H
        block = full.at[a, far, zi, yp]
        return remote(block, block, g3_s.at[a, zi, yp, h - 1], g3_r.at[a, zi, yp, h - 1], trow=x * H + far)

    def push_plane(a, d):
        for xp in range(C):
            away = jnp.logical_not(jnp.logical_and(diagonal, x == xp))

            @pl.when(away)
            def _():
                g2(a, d, xp).start()

    def split_block(a, half, zi, yp):
        value = full[a, half, zi, yp]
        high = value.astype(jnp.bfloat16)
        low = (value - high.astype(jnp.float32)).astype(jnp.bfloat16)
        at = pl.multiple_of((zi * C + yp) * rows, rows)
        lanes = pl.ds(pl.multiple_of(half * feats, feats), feats)
        vec[a % GROUPS, pl.ds(at, rows), lanes] = high
        vec[a % GROUPS, pl.ds(cols + at, rows), lanes] = low

    def land_plane(a, d):
        zi = block_of(d)
        for yp in range(C):
            here = jnp.logical_and(diagonal, y == yp)

            @pl.when(here)
            def _():
                full[a, c, zi, yp] = own[a, zi]

            @pl.when(jnp.logical_not(here))
            def _():
                g2_in(a, d, yp).wait_recv()

            for h in range(1, H):
                g3(a, d, yp, h).start()
            split_block(a, c, zi, yp)

    def land_core(a, d):
        zi = block_of(d)
        for yp in range(C):
            for h in range(1, H):
                g3_in(a, d, yp, h).wait_recv()
                split_block(a, (c + H - h) % H, zi, yp)

    def start_gather(a):
        pass_on(a, steps[0], lambda copy: copy.start())
        push_plane(a, steps[0])

    def arrive(a, step):
        zi = block_of(step)
        g1(a, zi, step[1]).wait_recv()
        pass_on(a, step, lambda copy: copy.start())
        push_plane(a, step)

    def finish_gather(a):
        count = len(steps)
        for i in range(count + 2):
            if 1 <= i < count:
                when(exists(steps[i]), lambda i=i: arrive(a, steps[i]))
            if 2 <= i + 1 <= count + 1 and 0 <= i - 1 < count:
                when(exists(steps[i - 1]), lambda i=i: land_plane(a, steps[i - 1]))
            if 0 <= i - 2 < count:
                when(exists(steps[i - 2]), lambda i=i: land_core(a, steps[i - 2]))
            yield

    def r1(a, n, dy):
        yp = (y + dy) % C
        return remote(prod.at[a, n, yp], from_y.at[a, n, dy], r1_s.at[a, n, dy - 1], r1_r.at[a, n, dy - 1], tcol=yp)

    def r2(a, n, d):
        zi = swap_bits(z, d)
        return remote(summed.at[a, n, zi], from_z.at[a, n, d], r2_s.at[a, n, d], r2_r.at[a, n, d], mp=zi)

    def multiply(a):
        @pl.loop(0, tiles)
        def _(n):
            at = pl.ds(pl.multiple_of(n * TILE, TILE), TILE)
            main = lax.dot_general(vec[a % GROUPS], g_hi[at, :], NT, preferred_element_type=jnp.float32)
            rest = lax.dot_general(vec[a % GROUPS, 0:cols, :], g_lo[at, :], NT, preferred_element_type=jnp.float32)
            total = main[0:cols] + (main[cols:2 * cols] + rest)
            for zi in range(Z):
                for yp in range(C):
                    row = (zi * C + yp) * rows
                    prod[a, n, yp, zi] = total[row:row + rows]

            @pl.when(n < 2)
            def _():
                for dy in range(1, C):
                    r1(a, n, dy).start()

    def scatter(a):
        for n in range(tiles):
            for dy in range(1, C):
                r1(a, n, dy).wait_recv()
                r1(a, n, dy).wait_send()
                if n + 2 < tiles:
                    r1(a, n + 2, dy).start()
            total = prod[a, n, y]
            for dy in range(1, C):
                total = total + from_y[a, n, dy]
            summed[a, n] = total
            for d in range(Z - 1, 0, -1):
                r2(a, n, d).start()
            yield
        for n in range(tiles):
            part = summed[a, n, z]
            for d in range(1, Z):
                r2(a, n, d).wait_recv()
                part = part + from_z[a, n, d]
            image[a % GROUPS, :, n * TILE:(n + 1) * TILE] = part
            yield

    def dot_copy(k, e):
        return remote(dots.at[k, t], dots.at[k, t], d_s.at[k, e], d_r.at[k, e], trow=(t + e) % T)

    def dot_in(k, e):
        far = (t + T - e) % T
        return remote(dots.at[k, far], dots.at[k, far], d_s.at[k, e], d_r.at[k, e], trow=far)

    def dot_start(k, value):
        dots[k, t] = jnp.broadcast_to(jnp.sum(value, axis=1, keepdims=True), (rows, 128))
        for e in range(1, T):
            dot_copy(k, e).start()

    def dot_finish(k):
        for e in range(1, T):
            dot_in(k, e).wait_recv()
        total = dots[k, 0]
        for e in range(1, T):
            total = total + dots[k, e]
        return total[:, 0:1]

    def band(g):
        return slice(g * rows, (g + 1) * rows)

    norms = {}

    def begin_update(b):
        a, g = b // GROUPS, b % GROUPS
        if a == 0:
            residual = rhs_ref[band(g)] - image[g]
            residual_ref[band(g)] = residual
            dirn[g] = residual
            own[b + GROUPS, z] = residual
            start_gather(b + GROUPS)
            dot_start(g, residual * residual)
            merged_ref[band(g)] = guess_ref[band(g)]
        else:
            dot_start((2 * a - 1) * GROUPS + g, dirn[g] * image[g])

    def finish_update(b):
        a, g = b // GROUPS, b % GROUPS
        if a == 0:
            return
        if a == 1:
            norms[g] = dot_finish(g)
        alpha = norms[g] / dot_finish((2 * a - 1) * GROUPS + g)
        residual = residual_ref[band(g)] - alpha * image[g]
        residual_ref[band(g)] = residual
        if a == ITERS:
            merged_ref[band(g)] = merged_ref[band(g)] + alpha * dirn[g]
            return
        k = 2 * a * GROUPS + g
        dot_start(k, residual * residual)
        merged_ref[band(g)] = merged_ref[band(g)] + alpha * dirn[g]
        yield
        norm_next = dot_finish(k)
        direction = residual_ref[band(g)] + (norm_next / norms[g]) * dirn[g]
        norms[g] = norm_next
        dirn[g] = direction
        own[b + GROUPS, z] = direction
        start_gather(b + GROUPS)
        yield

    def in_turns(*parts):
        parts = list(parts)
        while parts:
            for part in list(parts):
                try:
                    next(part)
                except StopIteration:
                    parts.remove(part)

    for g in range(GROUPS):
        own[g, z] = guess_ref[band(g)]
    for g in range(GROUPS):
        start_gather(g)
    for n in range(tiles):
        gram_copy(n).wait()

        @pl.loop(0, TILE // 32)
        def _(i):
            value = stage[n, pl.ds(pl.multiple_of(i * 32, 32), 32)]
            high = value.astype(jnp.bfloat16)
            at = pl.ds(pl.multiple_of(n * TILE + i * 32, 32), 32)
            g_hi[at, :] = high
            g_lo[at, :] = (value - high.astype(jnp.float32)).astype(jnp.bfloat16)

    turns = APPS * GROUPS

    def advance(b):
        if b >= GROUPS:
            yield from finish_update(b - GROUPS)
        if b < turns:
            yield from finish_gather(b)

    for b in range(GROUPS - 1):
        in_turns(advance(b))
    for b in range(turns):
        multiply(b)
        in_turns(advance(b + GROUPS - 1), scatter(b))
        begin_update(b)
    in_turns(advance(turns + GROUPS - 1))

    def end_block(a, step):
        pass_on(a, step, lambda copy: copy.wait_send())
        for xp in range(C):
            away = jnp.logical_not(jnp.logical_and(diagonal, x == xp))

            @pl.when(away)
            def _():
                g2(a, step, xp).wait_send()

            for h in range(1, H):
                g3(a, step, xp, h).wait_send()

    for a in range(turns):
        for step in steps:
            when(exists(step), lambda: end_block(a, step))
        for n in range(tiles):
            for d in range(1, Z):
                r2(a, n, d).wait_send()
    for k in range(2 * ITERS * GROUPS):
        for e in range(1, T):
            dot_copy(k, e).wait_send()


def kernel_shards(Z, T, C, gram, rhs, guess):
    H = T // C
    rows, feats = guess.shape[0] // GROUPS, guess.shape[1]
    tiles = feats // TILE
    turns = APPS * GROUPS
    cols = Z * C * rows
    f32, bf16 = jnp.float32, jnp.bfloat16
    dma = pltpu.SemaphoreType.DMA
    vmem = pl.BlockSpec(memory_space=pltpu.VMEM)
    shape = jax.ShapeDtypeStruct(guess.shape, f32)
    scratch = [
        pltpu.VMEM((tiles, TILE, H * feats), f32),
        pltpu.VMEM((feats, H * feats), bf16),
        pltpu.VMEM((feats, H * feats), bf16),
        pltpu.VMEM((GROUPS, 2 * cols, H * feats), bf16),
        pltpu.VMEM((turns, Z, rows, feats), f32),
        pltpu.VMEM((turns, H, Z, C, rows, feats), f32),
        pltpu.VMEM((turns, tiles, C, Z, rows, TILE), f32),
        pltpu.VMEM((turns, tiles, C, Z, rows, TILE), f32),
        pltpu.VMEM((turns, tiles, Z, rows, TILE), f32),
        pltpu.VMEM((turns, tiles, Z, rows, TILE), f32),
        pltpu.VMEM((2 * ITERS * GROUPS, T, rows, 128), f32),
        pltpu.VMEM((GROUPS, rows, feats), f32),
        pltpu.VMEM((GROUPS, rows, feats), f32),
        dma((tiles,)),
        dma((turns, 2, Z)), dma((turns, Z)),
        dma((turns, Z, C)), dma((turns, Z, C)),
        dma((turns, Z, C, H - 1)), dma((turns, Z, C, H - 1)),
        dma((turns, tiles, C - 1)), dma((turns, tiles, C - 1)),
        dma((turns, tiles, Z)), dma((turns, tiles, Z)),
        dma((2 * ITERS * GROUPS, T)), dma((2 * ITERS * GROUPS, T)),
    ]
    return pl.pallas_call(
        functools.partial(kernel, Z, T, C),
        out_shape=(shape, shape),
        in_specs=[pl.BlockSpec(memory_space=pl.ANY), vmem, vmem],
        out_specs=(vmem, vmem),
        scratch_shapes=scratch,
        cost_estimate=pl.CostEstimate(
            flops=turns * 6 * cols * feats * H * feats,
            bytes_accessed=gram.size * 4,
            transcendentals=0),
        compiler_params=pltpu.CompilerParams(
            collective_id=0, has_side_effects=True, vmem_limit_bytes=56 * 1024 * 1024),
    )(gram, rhs, guess)


def general_shards(gram, rhs, guess):
    gram_tile = gram[0]
    block_cols = gram_tile.shape[1]

    def apply_total(vector):
        columns = lax.all_gather(vector, ("mp", "tcol"), axis=0, tiled=True)
        gathered = lax.all_gather(columns, "trow", axis=1, tiled=True)
        block = lax.dynamic_slice_in_dim(
            gathered, lax.axis_index("tcol") * block_cols, block_cols, 1)
        terms = lax.dot_general(block, gram_tile, NT, precision=lax.Precision.HIGHEST,
                                preferred_element_type=jnp.float32)
        return lax.psum_scatter(terms, ("mp", "tcol"), scatter_dimension=0, tiled=True)

    def squares(values):
        return lax.psum(jnp.sum(values * values, axis=1), "trow")

    merged = guess
    residual = rhs - apply_total(guess)
    direction = residual
    norm_now = squares(residual)
    for step in range(ITERS):
        image = apply_total(direction)
        curve = lax.psum(jnp.sum(direction * image, axis=1), "trow")
        alpha = norm_now / curve
        merged = merged + alpha[:, None] * direction
        residual = residual - alpha[:, None] * image
        if step + 1 < ITERS:
            norm_next = squares(residual)
            direction = residual + (norm_next / norm_now)[:, None] * direction
            norm_now = norm_next
    return (merged, residual)


def solution(mesh):
    Z, T, C = mesh.shape["mp"], mesh.shape["trow"], mesh.shape["tcol"]

    def shards(gram, rhs, guess):
        rows, feats = guess.shape
        fits = T % C == 0 and Z & (Z - 1) == 0 and rows % (16 * GROUPS) == 0 and feats % TILE == 0
        fits = fits and T > C > 1 and Z > 1 and Z * C * rows * feats <= 256 * 1024 and gram.shape[0] == 1
        if fits:
            return kernel_shards(Z, T, C, gram, rhs, guess)
        return general_shards(gram, rhs, guess)

    in_specs = (P("mp", "trow", "tcol"), P(("mp", "tcol"), "trow"), P(("mp", "tcol"), "trow"))
    out_specs = (P(("mp", "tcol"), "trow"), P(("mp", "tcol"), "trow"))
    return jax.shard_map(shards, mesh=mesh, in_specs=in_specs, out_specs=out_specs, check_vma=False)
```

```python
import functools

import jax
import jax.numpy as jnp
from jax import lax
from jax.experimental import pallas as pl
from jax.experimental.pallas import tpu as pltpu
from jax.sharding import PartitionSpec as P

ITERS = 2
APPS = ITERS + 1
TILE = 256
MESH = pl.DeviceIdType.MESH
NT = (((1,), (1,)), ((), ()))
NN = (((1,), (0,)), ((), ()))


def swap_bits(index, bits):
    weight = 1
    out = index
    while weight <= bits:
        if (bits // weight) % 2:
            out = out + weight - 2 * weight * ((index // weight) % 2)
        weight *= 2
    return out


def kernel(Z, T, C, gram_ref, rhs_ref, guess_ref, merged_ref, residual_ref,
           stage, g_hi, g_lo, vec, own, full, prod, from_y, summed, from_z, dots, dirn, image,
           stage_sem, g1_s, g1_r, g2_s, g2_r, g3_s, g3_r, r1_s, r1_r, r2_s, r2_r, d_s, d_r):
    H = T // C
    rows, feats = guess_ref.shape
    tiles = feats // TILE
    cols = Z * C * rows
    z, t, y = lax.axis_index("mp"), lax.axis_index("trow"), lax.axis_index("tcol")
    x, c = t // H, t % H
    diagonal = x == y

    def gram_copy(n):
        return pltpu.make_async_copy(
            gram_ref.at[0, pl.ds(n * TILE, TILE)], stage.at[n], stage_sem.at[n])

    for n in range(tiles):
        gram_copy(n).start()

    def remote(src, dst, s_sem, r_sem, mp=None, trow=None, tcol=None):
        return pltpu.make_async_remote_copy(
            src_ref=src, dst_ref=dst, send_sem=s_sem, recv_sem=r_sem,
            device_id=(z if mp is None else mp, t if trow is None else trow,
                       y if tcol is None else tcol),
            device_id_type=MESH)

    barrier = pltpu.get_barrier_semaphore()
    for d in range(1, Z):
        pl.semaphore_signal(barrier, inc=1, device_id=(swap_bits(z, d), t, y), device_id_type=MESH)
    for e in range(1, T * C):
        place = (t * C + y + e) % (T * C)
        pl.semaphore_signal(barrier, inc=1, device_id=(z, place // C, place % C), device_id_type=MESH)
    pl.semaphore_wait(barrier, Z - 1 + T * C - 1)

    steps = [(0, 0)] + [(k, side) for k in range(1, Z) for side in (-1, 1)]

    def block_of(step):
        return z + step[0] * step[1]

    def exists(step):
        if step[0] == 0:
            return True
        return z >= step[0] if step[1] < 0 else z + step[0] < Z

    def when(condition, act):
        if condition is True:
            act()
        else:
            pl.when(condition)(act)

    def g1(a, zi, way):
        block = own.at[a, zi]
        return remote(block, block, g1_s.at[a, (way + 1) // 2, zi], g1_r.at[a, zi], mp=z + way)

    def pass_on(a, step, act):
        zi = block_of(step)
        for way in (-1, 1):
            if step[0] == 0 or step[1] == -way:
                more = z > 0 if way < 0 else z < Z - 1
                if step[0]:
                    more = jnp.logical_and(more, exists(step))
                when(more, lambda way=way: act(g1(a, zi, way)))

    def g2(a, d, xp):
        zi = block_of(d)
        return remote(own.at[a, zi], full.at[a, c, zi, y], g2_s.at[a, zi, xp], g2_r.at[a, zi, y],
                      trow=xp * H + c, tcol=x)

    def g2_in(a, d, yp):
        zi = block_of(d)
        return remote(own.at[a, zi], full.at[a, c, zi, yp], g2_s.at[a, zi, yp], g2_r.at[a, zi, yp],
                      trow=y * H + c, tcol=yp)

    def g3(a, d, yp, h):
        zi = block_of(d)
        block = full.at[a, c, zi, yp]
        return remote(block, block, g3_s.at[a, zi, yp, h], g3_r.at[a, zi, yp, h],
                      trow=x * H + (c + h) % H)

    def g3_in(a, d, yp, h):
        zi = block_of(d)
        far = (c + H - h) % H
        block = full.at[a, far, zi, yp]
        return remote(block, block, g3_s.at[a, zi, yp, h], g3_r.at[a, zi, yp, h], trow=x * H + far)

    def push_plane(a, d):
        for xp in range(C):
            away = jnp.logical_not(jnp.logical_and(diagonal, x == xp))

            @pl.when(away)
            def _():
                g2(a, d, xp).start()

    def split_block(a, half, zi, yp):
        value = full[a, half, zi, yp]
        high = value.astype(jnp.bfloat16)
        low = (value - high.astype(jnp.float32)).astype(jnp.bfloat16)
        at = pl.multiple_of((zi * C + yp) * rows, rows)
        lanes = pl.ds(pl.multiple_of(half * feats, feats), feats)
        vec[pl.ds(at, rows), lanes] = high
        vec[pl.ds(cols + at, rows), lanes] = low

    def land_plane(a, d):
        zi = block_of(d)
        for yp in range(C):
            here = jnp.logical_and(diagonal, y == yp)

            @pl.when(here)
            def _():
                full[a, c, zi, yp] = own[a, zi]

            @pl.when(jnp.logical_not(here))
            def _():
                g2_in(a, d, yp).wait_recv()

            for h in range(1, H):
                g3(a, d, yp, h).start()
            split_block(a, c, zi, yp)

    def land_core(a, d):
        zi = block_of(d)
        for yp in range(C):
            for h in range(1, H):
                g3_in(a, d, yp, h).wait_recv()
                split_block(a, (c + H - h) % H, zi, yp)

    def start_gather(a):
        pass_on(a, steps[0], lambda copy: copy.start())
        push_plane(a, steps[0])

    def arrive(a, step):
        zi = block_of(step)
        g1(a, zi, step[1]).wait_recv()
        pass_on(a, step, lambda copy: copy.start())
        push_plane(a, step)

    def finish_gather(a):
        count = len(steps)
        for i in range(count + 2):
            if 1 <= i < count:
                when(exists(steps[i]), lambda i=i: arrive(a, steps[i]))
            if 2 <= i + 1 <= count + 1 and 0 <= i - 1 < count:
                when(exists(steps[i - 1]), lambda i=i: land_plane(a, steps[i - 1]))
            if 0 <= i - 2 < count:
                when(exists(steps[i - 2]), lambda i=i: land_core(a, steps[i - 2]))
            yield

    def r1(a, n, dy):
        yp = (y + dy) % C
        return remote(prod.at[a, n, yp], from_y.at[a, n, dy], r1_s.at[a, n, dy], r1_r.at[a, n, dy], tcol=yp)

    def r2(a, n, d):
        zi = swap_bits(z, d)
        return remote(summed.at[a, n, zi], from_z.at[a, n, d], r2_s.at[a, n, d], r2_r.at[a, n, d], mp=zi)

    def multiply(a):
        @pl.loop(0, tiles)
        def _(n):
            main = lax.dot_general(vec[...], g_hi[n], NN, preferred_element_type=jnp.float32)
            rest = lax.dot_general(vec[0:cols, :], g_lo[n], NN, preferred_element_type=jnp.float32)
            total = main[0:cols] + (main[cols:2 * cols] + rest)
            for zi in range(Z):
                for yp in range(C):
                    row = (zi * C + yp) * rows
                    prod[a, n, yp, zi] = total[row:row + rows]

            @pl.when(n < 2)
            def _():
                for dy in range(1, C):
                    r1(a, n, dy).start()

    def scatter(a):
        for n in range(tiles):
            for dy in range(1, C):
                r1(a, n, dy).wait_recv()
                r1(a, n, dy).wait_send()
                if n + 2 < tiles:
                    r1(a, n + 2, dy).start()
            total = prod[a, n, y]
            for dy in range(1, C):
                total = total + from_y[a, n, dy]
            summed[a, n] = total
            for d in range(Z - 1, 0, -1):
                r2(a, n, d).start()
        for n in range(tiles):
            part = summed[a, n, z]
            for d in range(1, Z):
                r2(a, n, d).wait_recv()
                part = part + from_z[a, n, d]
            image[:, n * TILE:(n + 1) * TILE] = part

    def dot_copy(k, e):
        return remote(dots.at[k, t], dots.at[k, t], d_s.at[k, e], d_r.at[k, e], trow=(t + e) % T)

    def dot_in(k, e):
        far = (t + T - e) % T
        return remote(dots.at[k, far], dots.at[k, far], d_s.at[k, e], d_r.at[k, e], trow=far)

    def dot_start(k, value):
        dots[k, t] = jnp.broadcast_to(jnp.sum(value, axis=1, keepdims=True), (rows, 128))
        for e in range(1, T):
            dot_copy(k, e).start()

    def dot_finish(k):
        for e in range(1, T):
            dot_in(k, e).wait_recv()
        total = dots[k, 0]
        for e in range(1, T):
            total = total + dots[k, e]
        return total[:, 0:1]

    own[0, z] = guess_ref[...]
    start_gather(0)
    def in_turns(*parts):
        parts = list(parts)
        while parts:
            for part in list(parts):
                try:
                    next(part)
                except StopIteration:
                    parts.remove(part)

    def prepare():
        for n in range(tiles):
            gram_copy(n).wait()

            @pl.loop(0, H * feats // 256)
            def _(i):
                at = pl.ds(pl.multiple_of(i * 256, 256), 256)
                value = jnp.swapaxes(stage[n, :, at], 0, 1)
                high = value.astype(jnp.bfloat16)
                g_hi[n, at, :] = high
                g_lo[n, at, :] = (value - high.astype(jnp.float32)).astype(jnp.bfloat16)
            yield

    in_turns(finish_gather(0), prepare())
    multiply(0)
    scatter(0)
    residual = rhs_ref[...] - image[...]
    residual_ref[...] = residual
    own[1, z] = residual
    dirn[...] = residual
    merged_ref[...] = guess_ref[...]
    start_gather(1)
    dot_start(0, residual * residual)
    norm_now = None
    for step in range(ITERS):
        a = step + 1
        in_turns(finish_gather(a))
        multiply(a)
        scatter(a)
        dot_start(2 * step + 1, dirn[...] * image[...])
        if step == 0:
            norm_now = dot_finish(0)
        alpha = norm_now / dot_finish(2 * step + 1)
        residual = residual_ref[...] - alpha * image[...]
        residual_ref[...] = residual
        if step + 1 < ITERS:
            dot_start(2 * step + 2, residual * residual)
            merged_ref[...] = merged_ref[...] + alpha * dirn[...]
            norm_next = dot_finish(2 * step + 2)
            direction = residual + (norm_next / norm_now) * dirn[...]
            dirn[...] = direction
            own[a + 1, z] = direction
            start_gather(a + 1)
            norm_now = norm_next
        else:
            merged_ref[...] = merged_ref[...] + alpha * dirn[...]

    def end_block(a, step):
        pass_on(a, step, lambda copy: copy.wait_send())
        for xp in range(C):
            away = jnp.logical_not(jnp.logical_and(diagonal, x == xp))

            @pl.when(away)
            def _():
                g2(a, step, xp).wait_send()

            for h in range(1, H):
                g3(a, step, xp, h).wait_send()

    for a in range(APPS):
        for step in steps:
            when(exists(step), lambda: end_block(a, step))
        for n in range(tiles):
            for d in range(1, Z):
                r2(a, n, d).wait_send()
    for k in range(2 * ITERS):
        for e in range(1, T):
            dot_copy(k, e).wait_send()


def kernel_shards(Z, T, C, gram, rhs, guess):
    H = T // C
    rows, feats = guess.shape
    tiles = feats // TILE
    cols = Z * C * rows
    f32, bf16 = jnp.float32, jnp.bfloat16
    dma = pltpu.SemaphoreType.DMA
    vmem = pl.BlockSpec(memory_space=pltpu.VMEM)
    shape = jax.ShapeDtypeStruct(guess.shape, f32)
    scratch = [
        pltpu.VMEM((tiles, TILE, H * feats), f32),
        pltpu.VMEM((tiles, H * feats, TILE), bf16),
        pltpu.VMEM((tiles, H * feats, TILE), bf16),
        pltpu.VMEM((2 * cols, H * feats), bf16),
        pltpu.VMEM((APPS, Z, rows, feats), f32),
        pltpu.VMEM((APPS, H, Z, C, rows, feats), f32),
        pltpu.VMEM((APPS, tiles, C, Z, rows, TILE), f32),
        pltpu.VMEM((APPS, tiles, C, Z, rows, TILE), f32),
        pltpu.VMEM((APPS, tiles, Z, rows, TILE), f32),
        pltpu.VMEM((APPS, tiles, Z, rows, TILE), f32),
        pltpu.VMEM((2 * ITERS, T, rows, 128), f32),
        pltpu.VMEM((rows, feats), f32),
        pltpu.VMEM((rows, feats), f32),
        dma((tiles,)),
        dma((APPS, 2, Z)), dma((APPS, Z)),
        dma((APPS, Z, C)), dma((APPS, Z, C)),
        dma((APPS, Z, C, H)), dma((APPS, Z, C, H)),
        dma((APPS, tiles, C)), dma((APPS, tiles, C)),
        dma((APPS, tiles, Z)), dma((APPS, tiles, Z)),
        dma((2 * ITERS, T)), dma((2 * ITERS, T)),
    ]
    return pl.pallas_call(
        functools.partial(kernel, Z, T, C),
        out_shape=(shape, shape),
        in_specs=[pl.BlockSpec(memory_space=pl.ANY), vmem, vmem],
        out_specs=(vmem, vmem),
        scratch_shapes=scratch,
        cost_estimate=pl.CostEstimate(
            flops=APPS * 6 * cols * feats * H * feats,
            bytes_accessed=gram.size * 4,
            transcendentals=0),
        compiler_params=pltpu.CompilerParams(
            collective_id=0, has_side_effects=True, vmem_limit_bytes=56 * 1024 * 1024),
    )(gram, rhs, guess)


def general_shards(gram, rhs, guess):
    gram_tile = gram[0]
    block_cols = gram_tile.shape[1]

    def apply_total(vector):
        columns = lax.all_gather(vector, ("mp", "tcol"), axis=0, tiled=True)
        gathered = lax.all_gather(columns, "trow", axis=1, tiled=True)
        block = lax.dynamic_slice_in_dim(
            gathered, lax.axis_index("tcol") * block_cols, block_cols, 1)
        terms = lax.dot_general(block, gram_tile, NT, precision=lax.Precision.HIGHEST,
                                preferred_element_type=jnp.float32)
        return lax.psum_scatter(terms, ("mp", "tcol"), scatter_dimension=0, tiled=True)

    def squares(values):
        return lax.psum(jnp.sum(values * values, axis=1), "trow")

    merged = guess
    residual = rhs - apply_total(guess)
    direction = residual
    norm_now = squares(residual)
    for step in range(ITERS):
        image = apply_total(direction)
        curve = lax.psum(jnp.sum(direction * image, axis=1), "trow")
        alpha = norm_now / curve
        merged = merged + alpha[:, None] * direction
        residual = residual - alpha[:, None] * image
        if step + 1 < ITERS:
            norm_next = squares(residual)
            direction = residual + (norm_next / norm_now)[:, None] * direction
            norm_now = norm_next
    return (merged, residual)


def solution(mesh):
    Z, T, C = mesh.shape["mp"], mesh.shape["trow"], mesh.shape["tcol"]

    def shards(gram, rhs, guess):
        rows, feats = guess.shape
        fits = T % C == 0 and Z & (Z - 1) == 0 and rows % 16 == 0 and feats % TILE == 0
        fits = fits and Z * C * rows * feats <= 256 * 1024 and gram.shape[0] == 1
        if fits:
            return kernel_shards(Z, T, C, gram, rhs, guess)
        return general_shards(gram, rhs, guess)

    in_specs = (P("mp", "trow", "tcol"), P(("mp", "tcol"), "trow"), P(("mp", "tcol"), "trow"))
    out_specs = (P(("mp", "tcol"), "trow"), P(("mp", "tcol"), "trow"))
    return jax.shard_map(shards, mesh=mesh, in_specs=in_specs, out_specs=out_specs, check_vma=False)
```

```python
import functools

import jax
import jax.numpy as jnp
from jax import lax
from jax.experimental import pallas as pl
from jax.experimental.pallas import tpu as pltpu
from jax.sharding import PartitionSpec as P

ITERS = 2
APPS = ITERS + 1
TILE = 256
MESH = pl.DeviceIdType.MESH
NT = (((1,), (1,)), ((), ()))


def swap_bits(index, bits):
    weight = 1
    out = index
    while weight <= bits:
        if (bits // weight) % 2:
            out = out + weight - 2 * weight * ((index // weight) % 2)
        weight *= 2
    return out


def kernel(Z, T, C, gram_ref, rhs_ref, guess_ref, merged_ref, residual_ref,
           stage, g_hi, g_lo, vec, own, relay, full, prod, from_y, summed, from_z, dots, dirn, image,
           stage_sem, g1_s, g1_r, g2_s, g2_r, hop_s, hop_r, on_s, g3_s, g3_r, r1_s, r1_r, r2_s, r2_r, d_s, d_r):
    H = T // C
    rows, feats = guess_ref.shape
    tiles = feats // TILE
    cols = Z * C * rows
    z, t, y = lax.axis_index("mp"), lax.axis_index("trow"), lax.axis_index("tcol")
    x, c = t // H, t % H
    diagonal = x == y

    def gram_copy(n):
        return pltpu.make_async_copy(
            gram_ref.at[0, pl.ds(n * TILE, TILE)], stage.at[n], stage_sem.at[n])

    for n in range(tiles):
        gram_copy(n).start()

    def remote(src, dst, s_sem, r_sem, mp=None, trow=None, tcol=None):
        return pltpu.make_async_remote_copy(
            src_ref=src, dst_ref=dst, send_sem=s_sem, recv_sem=r_sem,
            device_id=(z if mp is None else mp, t if trow is None else trow,
                       y if tcol is None else tcol),
            device_id_type=MESH)

    barrier = pltpu.get_barrier_semaphore()
    for d in range(1, Z):
        pl.semaphore_signal(barrier, inc=1, device_id=(swap_bits(z, d), t, y), device_id_type=MESH)
    for e in range(1, T * C):
        place = (t * C + y + e) % (T * C)
        pl.semaphore_signal(barrier, inc=1, device_id=(z, place // C, place % C), device_id_type=MESH)
    pl.semaphore_wait(barrier, Z - 1 + T * C - 1)

    steps = [(0, 0)] + [(k, side) for k in range(1, Z) for side in (-1, 1)]

    def block_of(step):
        return z + step[0] * step[1]

    def exists(step):
        if step[0] == 0:
            return True
        return z >= step[0] if step[1] < 0 else z + step[0] < Z

    def when(condition, act):
        if condition is True:
            act()
        else:
            pl.when(condition)(act)

    def g1(a, zi, way):
        block = own.at[a, zi]
        return remote(block, block, g1_s.at[a, (way + 1) // 2, zi], g1_r.at[a, zi], mp=z + way)

    def pass_on(a, step, act):
        zi = block_of(step)
        for way in (-1, 1):
            if step[0] == 0 or step[1] == -way:
                more = z > 0 if way < 0 else z < Z - 1
                if step[0]:
                    more = jnp.logical_and(more, exists(step))
                when(more, lambda way=way: act(g1(a, zi, way)))

    def g2(a, d, xp):
        zi = block_of(d)
        return remote(own.at[a, zi], full.at[a, c, zi, y], g2_s.at[a, zi, xp], g2_r.at[a, zi, y],
                      trow=xp * H + c, tcol=x)

    def g2_in(a, d, yp):
        zi = block_of(d)
        return remote(own.at[a, zi], full.at[a, c, zi, yp], g2_s.at[a, zi, yp], g2_r.at[a, zi, yp],
                      trow=y * H + c, tcol=yp)

    def g3(a, d, yp, h):
        zi = block_of(d)
        block = full.at[a, c, zi, yp]
        return remote(block, block, g3_s.at[a, zi, yp, h], g3_r.at[a, zi, yp, h],
                      trow=x * H + (c + h) % H)

    def g3_in(a, d, yp, h):
        zi = block_of(d)
        far = (c + H - h) % H
        block = full.at[a, far, zi, yp]
        return remote(block, block, g3_s.at[a, zi, yp, h], g3_r.at[a, zi, yp, h], trow=x * H + far)

    def hop(a, d):
        zi = block_of(d)
        return remote(own.at[a, zi], relay.at[a, zi], hop_s.at[a, zi], hop_r.at[a, zi], trow=(1 - x) * H + c)

    def onward(a, d):
        zi = block_of(d)
        return remote(relay.at[a, zi], full.at[a, c, zi, y], on_s.at[a, zi], g2_r.at[a, zi, y], tcol=1 - y)

    def push_plane(a, d):
        @pl.when(diagonal)
        def _():
            g2(a, d, 1 - x).start()

        @pl.when(jnp.logical_not(diagonal))
        def _():
            hop(a, d).start()
            g2(a, d, x).start()

    def split_block(a, half, zi, yp):
        value = full[a, half, zi, yp]
        high = value.astype(jnp.bfloat16)
        low = (value - high.astype(jnp.float32)).astype(jnp.bfloat16)
        at = pl.multiple_of((zi * C + yp) * rows, rows)
        lanes = pl.ds(pl.multiple_of(half * feats, feats), feats)
        vec[pl.ds(at, rows), lanes] = high
        vec[pl.ds(cols + at, rows), lanes] = low

    def land_plane(a, d):
        zi = block_of(d)

        @pl.when(diagonal)
        def _():
            hop(a, d).wait_recv()
            onward(a, d).start()

        for yp in range(C):
            here = jnp.logical_and(diagonal, y == yp)

            @pl.when(here)
            def _():
                full[a, c, zi, yp] = own[a, zi]

            @pl.when(jnp.logical_not(here))
            def _():
                g2_in(a, d, yp).wait_recv()

            for h in range(1, H):
                g3(a, d, yp, h).start()
            split_block(a, c, zi, yp)

    def land_core(a, d):
        zi = block_of(d)
        for yp in range(C):
            for h in range(1, H):
                g3_in(a, d, yp, h).wait_recv()
                split_block(a, (c + H - h) % H, zi, yp)

    def start_gather(a):
        pass_on(a, steps[0], lambda copy: copy.start())
        push_plane(a, steps[0])

    def arrive(a, step):
        zi = block_of(step)
        g1(a, zi, step[1]).wait_recv()
        pass_on(a, step, lambda copy: copy.start())
        push_plane(a, step)

    def finish_gather(a):
        count = len(steps)
        for i in range(count + 2):
            if 1 <= i < count:
                when(exists(steps[i]), lambda i=i: arrive(a, steps[i]))
            if 2 <= i + 1 <= count + 1 and 0 <= i - 1 < count:
                when(exists(steps[i - 1]), lambda i=i: land_plane(a, steps[i - 1]))
            if 0 <= i - 2 < count:
                when(exists(steps[i - 2]), lambda i=i: land_core(a, steps[i - 2]))

    def r1(a, n, dy):
        yp = (y + dy) % C
        return remote(prod.at[a, n, yp], from_y.at[a, n, dy], r1_s.at[a, n, dy], r1_r.at[a, n, dy], tcol=yp)

    def r2(a, n, d):
        zi = swap_bits(z, d)
        return remote(summed.at[a, n, zi], from_z.at[a, n, d], r2_s.at[a, n, d], r2_r.at[a, n, d], mp=zi)

    def multiply(a):
        @pl.loop(0, tiles)
        def _(n):
            at = pl.ds(pl.multiple_of(n * TILE, TILE), TILE)
            main = lax.dot_general(vec[...], g_hi[at, :], NT, preferred_element_type=jnp.float32)
            rest = lax.dot_general(vec[0:cols, :], g_lo[at, :], NT, preferred_element_type=jnp.float32)
            total = main[0:cols] + (main[cols:2 * cols] + rest)
            for zi in range(Z):
                for yp in range(C):
                    row = (zi * C + yp) * rows
                    prod[a, n, yp, zi] = total[row:row + rows]

            @pl.when(n < 2)
            def _():
                for dy in range(1, C):
                    r1(a, n, dy).start()

    def scatter(a):
        for n in range(tiles):
            for dy in range(1, C):
                r1(a, n, dy).wait_recv()
                r1(a, n, dy).wait_send()
                if n + 2 < tiles:
                    r1(a, n + 2, dy).start()
            total = prod[a, n, y]
            for dy in range(1, C):
                total = total + from_y[a, n, dy]
            summed[a, n] = total
            for d in range(Z - 1, 0, -1):
                r2(a, n, d).start()
        for n in range(tiles):
            part = summed[a, n, z]
            for d in range(1, Z):
                r2(a, n, d).wait_recv()
                part = part + from_z[a, n, d]
            image[:, n * TILE:(n + 1) * TILE] = part

    def dot_copy(k, e):
        return remote(dots.at[k, t], dots.at[k, t], d_s.at[k, e], d_r.at[k, e], trow=(t + e) % T)

    def dot_in(k, e):
        far = (t + T - e) % T
        return remote(dots.at[k, far], dots.at[k, far], d_s.at[k, e], d_r.at[k, e], trow=far)

    def dot_start(k, value):
        dots[k, t] = jnp.broadcast_to(jnp.sum(value, axis=1, keepdims=True), (rows, 128))
        for e in range(1, T):
            dot_copy(k, e).start()

    def dot_finish(k):
        for e in range(1, T):
            dot_in(k, e).wait_recv()
        total = dots[k, 0]
        for e in range(1, T):
            total = total + dots[k, e]
        return total[:, 0:1]

    own[0, z] = guess_ref[...]
    start_gather(0)
    for n in range(tiles):
        gram_copy(n).wait()

        @pl.loop(0, TILE // 32)
        def _(i):
            value = stage[n, pl.ds(pl.multiple_of(i * 32, 32), 32)]
            high = value.astype(jnp.bfloat16)
            at = pl.ds(pl.multiple_of(n * TILE + i * 32, 32), 32)
            g_hi[at, :] = high
            g_lo[at, :] = (value - high.astype(jnp.float32)).astype(jnp.bfloat16)

    finish_gather(0)
    multiply(0)
    scatter(0)
    residual = rhs_ref[...] - image[...]
    residual_ref[...] = residual
    own[1, z] = residual
    dirn[...] = residual
    merged_ref[...] = guess_ref[...]
    start_gather(1)
    dot_start(0, residual * residual)
    norm_now = None
    for step in range(ITERS):
        a = step + 1
        finish_gather(a)
        multiply(a)
        scatter(a)
        dot_start(2 * step + 1, dirn[...] * image[...])
        if step == 0:
            norm_now = dot_finish(0)
        alpha = norm_now / dot_finish(2 * step + 1)
        residual = residual_ref[...] - alpha * image[...]
        residual_ref[...] = residual
        if step + 1 < ITERS:
            dot_start(2 * step + 2, residual * residual)
            merged_ref[...] = merged_ref[...] + alpha * dirn[...]
            norm_next = dot_finish(2 * step + 2)
            direction = residual + (norm_next / norm_now) * dirn[...]
            dirn[...] = direction
            own[a + 1, z] = direction
            start_gather(a + 1)
            norm_now = norm_next
        else:
            merged_ref[...] = merged_ref[...] + alpha * dirn[...]

    def end_block(a, step):
        pass_on(a, step, lambda copy: copy.wait_send())
        @pl.when(diagonal)
        def _():
            g2(a, step, 1 - x).wait_send()
            onward(a, step).wait_send()

        @pl.when(jnp.logical_not(diagonal))
        def _():
            hop(a, step).wait_send()
            g2(a, step, x).wait_send()

        for xp in range(C):
            for h in range(1, H):
                g3(a, step, xp, h).wait_send()

    for a in range(APPS):
        for step in steps:
            when(exists(step), lambda: end_block(a, step))
        for n in range(tiles):
            for d in range(1, Z):
                r2(a, n, d).wait_send()
    for k in range(2 * ITERS):
        for e in range(1, T):
            dot_copy(k, e).wait_send()


def kernel_shards(Z, T, C, gram, rhs, guess):
    H = T // C
    rows, feats = guess.shape
    tiles = feats // TILE
    cols = Z * C * rows
    f32, bf16 = jnp.float32, jnp.bfloat16
    dma = pltpu.SemaphoreType.DMA
    vmem = pl.BlockSpec(memory_space=pltpu.VMEM)
    shape = jax.ShapeDtypeStruct(guess.shape, f32)
    scratch = [
        pltpu.VMEM((tiles, TILE, H * feats), f32),
        pltpu.VMEM((feats, H * feats), bf16),
        pltpu.VMEM((feats, H * feats), bf16),
        pltpu.VMEM((2 * cols, H * feats), bf16),
        pltpu.VMEM((APPS, Z, rows, feats), f32),
        pltpu.VMEM((APPS, Z, rows, feats), f32),
        pltpu.VMEM((APPS, H, Z, C, rows, feats), f32),
        pltpu.VMEM((APPS, tiles, C, Z, rows, TILE), f32),
        pltpu.VMEM((APPS, tiles, C, Z, rows, TILE), f32),
        pltpu.VMEM((APPS, tiles, Z, rows, TILE), f32),
        pltpu.VMEM((APPS, tiles, Z, rows, TILE), f32),
        pltpu.VMEM((2 * ITERS, T, rows, 128), f32),
        pltpu.VMEM((rows, feats), f32),
        pltpu.VMEM((rows, feats), f32),
        dma((tiles,)),
        dma((APPS, 2, Z)), dma((APPS, Z)),
        dma((APPS, Z, C)), dma((APPS, Z, C)),
        dma((APPS, Z)), dma((APPS, Z)), dma((APPS, Z)),
        dma((APPS, Z, C, H)), dma((APPS, Z, C, H)),
        dma((APPS, tiles, C)), dma((APPS, tiles, C)),
        dma((APPS, tiles, Z)), dma((APPS, tiles, Z)),
        dma((2 * ITERS, T)), dma((2 * ITERS, T)),
    ]
    return pl.pallas_call(
        functools.partial(kernel, Z, T, C),
        out_shape=(shape, shape),
        in_specs=[pl.BlockSpec(memory_space=pl.ANY), vmem, vmem],
        out_specs=(vmem, vmem),
        scratch_shapes=scratch,
        cost_estimate=pl.CostEstimate(
            flops=APPS * 6 * cols * feats * H * feats,
            bytes_accessed=gram.size * 4,
            transcendentals=0),
        compiler_params=pltpu.CompilerParams(
            collective_id=0, has_side_effects=True, vmem_limit_bytes=56 * 1024 * 1024),
    )(gram, rhs, guess)


def general_shards(gram, rhs, guess):
    gram_tile = gram[0]
    block_cols = gram_tile.shape[1]

    def apply_total(vector):
        columns = lax.all_gather(vector, ("mp", "tcol"), axis=0, tiled=True)
        gathered = lax.all_gather(columns, "trow", axis=1, tiled=True)
        block = lax.dynamic_slice_in_dim(
            gathered, lax.axis_index("tcol") * block_cols, block_cols, 1)
        terms = lax.dot_general(block, gram_tile, NT, precision=lax.Precision.HIGHEST,
                                preferred_element_type=jnp.float32)
        return lax.psum_scatter(terms, ("mp", "tcol"), scatter_dimension=0, tiled=True)

    def squares(values):
        return lax.psum(jnp.sum(values * values, axis=1), "trow")

    merged = guess
    residual = rhs - apply_total(guess)
    direction = residual
    norm_now = squares(residual)
    for step in range(ITERS):
        image = apply_total(direction)
        curve = lax.psum(jnp.sum(direction * image, axis=1), "trow")
        alpha = norm_now / curve
        merged = merged + alpha[:, None] * direction
        residual = residual - alpha[:, None] * image
        if step + 1 < ITERS:
            norm_next = squares(residual)
            direction = residual + (norm_next / norm_now)[:, None] * direction
            norm_now = norm_next
    return (merged, residual)


def solution(mesh):
    Z, T, C = mesh.shape["mp"], mesh.shape["trow"], mesh.shape["tcol"]

    def shards(gram, rhs, guess):
        rows, feats = guess.shape
        fits = T % C == 0 and C == 2 and T == C * (T // C) and Z & (Z - 1) == 0 and rows % 16 == 0 and feats % TILE == 0
        fits = fits and Z * C * rows * feats <= 256 * 1024 and gram.shape[0] == 1
        if fits:
            return kernel_shards(Z, T, C, gram, rhs, guess)
        return general_shards(gram, rhs, guess)

    in_specs = (P("mp", "trow", "tcol"), P(("mp", "tcol"), "trow"), P(("mp", "tcol"), "trow"))
    out_specs = (P(("mp", "tcol"), "trow"), P(("mp", "tcol"), "trow"))
    return jax.shard_map(shards, mesh=mesh, in_specs=in_specs, out_specs=out_specs, check_vma=False)
```

```python
import functools

import jax
import jax.numpy as jnp
from jax import lax
from jax.experimental import pallas as pl
from jax.experimental.pallas import tpu as pltpu
from jax.sharding import PartitionSpec as P

ITERS = 2
APPS = ITERS + 1
TILE = 256
MESH = pl.DeviceIdType.MESH
NT = (((1,), (1,)), ((), ()))


def swap_bits(index, bits):
    weight = 1
    out = index
    while weight <= bits:
        if (bits // weight) % 2:
            out = out + weight - 2 * weight * ((index // weight) % 2)
        weight *= 2
    return out


def kernel(Z, T, C, gram_ref, rhs_ref, guess_ref, merged_ref, residual_ref,
           stage, g_hi, g_lo, vec, own, full, prod, from_y, summed, from_z, dots, dirn, image,
           stage_sem, g1_s, g1_r, g2_s, g2_r, g3_s, g3_r, r1_s, r1_r, r2_s, r2_r, d_s, d_r):
    H = T // C
    rows, feats = guess_ref.shape
    tiles = feats // TILE
    cols = Z * C * rows
    z, t, y = lax.axis_index("mp"), lax.axis_index("trow"), lax.axis_index("tcol")
    x, c = t // H, t % H
    diagonal = x == y

    def gram_copy(n):
        return pltpu.make_async_copy(
            gram_ref.at[0, pl.ds(n * TILE, TILE)], stage.at[n], stage_sem.at[n])

    for n in range(tiles):
        gram_copy(n).start()

    def remote(src, dst, s_sem, r_sem, mp=None, trow=None, tcol=None):
        return pltpu.make_async_remote_copy(
            src_ref=src, dst_ref=dst, send_sem=s_sem, recv_sem=r_sem,
            device_id=(z if mp is None else mp, t if trow is None else trow,
                       y if tcol is None else tcol),
            device_id_type=MESH)

    barrier = pltpu.get_barrier_semaphore()
    for d in range(1, Z):
        pl.semaphore_signal(barrier, inc=1, device_id=(swap_bits(z, d), t, y), device_id_type=MESH)
    for e in range(1, T * C):
        place = (t * C + y + e) % (T * C)
        pl.semaphore_signal(barrier, inc=1, device_id=(z, place // C, place % C), device_id_type=MESH)
    pl.semaphore_wait(barrier, Z - 1 + T * C - 1)

    steps = [(0, 0)] + [(k, side) for k in range(1, Z) for side in (-1, 1)]

    def block_of(step):
        return z + step[0] * step[1]

    def exists(step):
        if step[0] == 0:
            return True
        return z >= step[0] if step[1] < 0 else z + step[0] < Z

    def when(condition, act):
        if condition is True:
            act()
        else:
            pl.when(condition)(act)

    def g1(a, zi, way):
        block = own.at[a, zi]
        return remote(block, block, g1_s.at[a, (way + 1) // 2, zi], g1_r.at[a, zi], mp=z + way)

    def pass_on(a, step, act):
        zi = block_of(step)
        for way in (-1, 1):
            if step[0] == 0 or step[1] == -way:
                more = z > 0 if way < 0 else z < Z - 1
                if step[0]:
                    more = jnp.logical_and(more, exists(step))
                when(more, lambda way=way: act(g1(a, zi, way)))

    def g2(a, d, xp):
        zi = block_of(d)
        return remote(own.at[a, zi], full.at[a, c, zi, y], g2_s.at[a, zi, xp], g2_r.at[a, zi, y],
                      trow=xp * H + c, tcol=x)

    def g2_in(a, d, yp):
        zi = block_of(d)
        return remote(own.at[a, zi], full.at[a, c, zi, yp], g2_s.at[a, zi, yp], g2_r.at[a, zi, yp],
                      trow=y * H + c, tcol=yp)

    def g3(a, d, yp, h):
        zi = block_of(d)
        block = full.at[a, c, zi, yp]
        return remote(block, block, g3_s.at[a, zi, yp, h], g3_r.at[a, zi, yp, h],
                      trow=x * H + (c + h) % H)

    def g3_in(a, d, yp, h):
        zi = block_of(d)
        far = (c + H - h) % H
        block = full.at[a, far, zi, yp]
        return remote(block, block, g3_s.at[a, zi, yp, h], g3_r.at[a, zi, yp, h], trow=x * H + far)

    def push_plane(a, d):
        for xp in range(C):
            away = jnp.logical_not(jnp.logical_and(diagonal, x == xp))

            @pl.when(away)
            def _():
                g2(a, d, xp).start()

    def split_block(a, half, zi, yp):
        value = full[a, half, zi, yp]
        high = value.astype(jnp.bfloat16)
        low = (value - high.astype(jnp.float32)).astype(jnp.bfloat16)
        at = pl.multiple_of((zi * C + yp) * rows, rows)
        lanes = pl.ds(pl.multiple_of(half * feats, feats), feats)
        vec[pl.ds(at, rows), lanes] = high
        vec[pl.ds(cols + at, rows), lanes] = low

    def land_plane(a, d):
        zi = block_of(d)
        for yp in range(C):
            here = jnp.logical_and(diagonal, y == yp)

            @pl.when(here)
            def _():
                full[a, c, zi, yp] = own[a, zi]

            @pl.when(jnp.logical_not(here))
            def _():
                g2_in(a, d, yp).wait_recv()

            for h in range(1, H):
                g3(a, d, yp, h).start()
            split_block(a, c, zi, yp)

    def land_core(a, d):
        zi = block_of(d)
        for yp in range(C):
            for h in range(1, H):
                g3_in(a, d, yp, h).wait_recv()
                split_block(a, (c + H - h) % H, zi, yp)

    def start_gather(a):
        pass_on(a, steps[0], lambda copy: copy.start())
        push_plane(a, steps[0])

    def arrive(a, step):
        zi = block_of(step)
        g1(a, zi, step[1]).wait_recv()
        pass_on(a, step, lambda copy: copy.start())
        push_plane(a, step)

    def finish_gather(a):
        for step in steps[1:]:
            when(exists(step), lambda: arrive(a, step))
        for i in range(len(steps) + 1):
            if i < len(steps):
                when(exists(steps[i]), lambda: land_plane(a, steps[i]))
            if i >= 1:
                when(exists(steps[i - 1]), lambda: land_core(a, steps[i - 1]))

    def r1(a, n, dy):
        yp = (y + dy) % C
        return remote(prod.at[a, n, yp], from_y.at[a, n, dy], r1_s.at[a, n, dy], r1_r.at[a, n, dy], tcol=yp)

    def r2(a, n, d):
        zi = swap_bits(z, d)
        return remote(summed.at[a, n, zi], from_z.at[a, n, d], r2_s.at[a, n, d], r2_r.at[a, n, d], mp=zi)

    def multiply(a):
        @pl.loop(0, tiles)
        def _(n):
            at = pl.ds(pl.multiple_of(n * TILE, TILE), TILE)
            main = lax.dot_general(vec[...], g_hi[at, :], NT, preferred_element_type=jnp.float32)
            rest = lax.dot_general(vec[0:cols, :], g_lo[at, :], NT, preferred_element_type=jnp.float32)
            total = main[0:cols] + (main[cols:2 * cols] + rest)
            for zi in range(Z):
                for yp in range(C):
                    row = (zi * C + yp) * rows
                    prod[a, n, yp, zi] = total[row:row + rows]

            @pl.when(n < 2)
            def _():
                for dy in range(1, C):
                    r1(a, n, dy).start()

    def scatter(a):
        for n in range(tiles):
            for dy in range(1, C):
                r1(a, n, dy).wait_recv()
                r1(a, n, dy).wait_send()
                if n + 2 < tiles:
                    r1(a, n + 2, dy).start()
            total = prod[a, n, y]
            for dy in range(1, C):
                total = total + from_y[a, n, dy]
            summed[a, n] = total
            for d in range(Z - 1, 0, -1):
                r2(a, n, d).start()
        for n in range(tiles):
            part = summed[a, n, z]
            for d in range(1, Z):
                r2(a, n, d).wait_recv()
                part = part + from_z[a, n, d]
            image[:, n * TILE:(n + 1) * TILE] = part

    def dot_copy(k, e):
        return remote(dots.at[k, t], dots.at[k, t], d_s.at[k, e], d_r.at[k, e], trow=(t + e) % T)

    def dot_in(k, e):
        far = (t + T - e) % T
        return remote(dots.at[k, far], dots.at[k, far], d_s.at[k, e], d_r.at[k, e], trow=far)

    def dot_start(k, value):
        dots[k, t] = jnp.broadcast_to(jnp.sum(value, axis=1, keepdims=True), (rows, 128))
        for e in range(1, T):
            dot_copy(k, e).start()

    def dot_finish(k):
        for e in range(1, T):
            dot_in(k, e).wait_recv()
        total = dots[k, 0]
        for e in range(1, T):
            total = total + dots[k, e]
        return total[:, 0:1]

    own[0, z] = guess_ref[...]
    start_gather(0)
    for n in range(tiles):
        gram_copy(n).wait()

        @pl.loop(0, TILE // 32)
        def _(i):
            value = stage[n, pl.ds(pl.multiple_of(i * 32, 32), 32)]
            high = value.astype(jnp.bfloat16)
            at = pl.ds(pl.multiple_of(n * TILE + i * 32, 32), 32)
            g_hi[at, :] = high
            g_lo[at, :] = (value - high.astype(jnp.float32)).astype(jnp.bfloat16)

    finish_gather(0)
    multiply(0)
    scatter(0)
    residual = rhs_ref[...] - image[...]
    residual_ref[...] = residual
    own[1, z] = residual
    dirn[...] = residual
    merged_ref[...] = guess_ref[...]
    start_gather(1)
    dot_start(0, residual * residual)
    norm_now = None
    for step in range(ITERS):
        a = step + 1
        finish_gather(a)
        multiply(a)
        scatter(a)
        dot_start(2 * step + 1, dirn[...] * image[...])
        if step == 0:
            norm_now = dot_finish(0)
        alpha = norm_now / dot_finish(2 * step + 1)
        residual = residual_ref[...] - alpha * image[...]
        residual_ref[...] = residual
        if step + 1 < ITERS:
            dot_start(2 * step + 2, residual * residual)
            merged_ref[...] = merged_ref[...] + alpha * dirn[...]
            norm_next = dot_finish(2 * step + 2)
            direction = residual + (norm_next / norm_now) * dirn[...]
            dirn[...] = direction
            own[a + 1, z] = direction
            start_gather(a + 1)
            norm_now = norm_next
        else:
            merged_ref[...] = merged_ref[...] + alpha * dirn[...]

    def end_block(a, step):
        pass_on(a, step, lambda copy: copy.wait_send())
        for xp in range(C):
            away = jnp.logical_not(jnp.logical_and(diagonal, x == xp))

            @pl.when(away)
            def _():
                g2(a, step, xp).wait_send()

            for h in range(1, H):
                g3(a, step, xp, h).wait_send()

    for a in range(APPS):
        for step in steps:
            when(exists(step), lambda: end_block(a, step))
        for n in range(tiles):
            for d in range(1, Z):
                r2(a, n, d).wait_send()
    for k in range(2 * ITERS):
        for e in range(1, T):
            dot_copy(k, e).wait_send()


def kernel_shards(Z, T, C, gram, rhs, guess):
    H = T // C
    rows, feats = guess.shape
    tiles = feats // TILE
    cols = Z * C * rows
    f32, bf16 = jnp.float32, jnp.bfloat16
    dma = pltpu.SemaphoreType.DMA
    vmem = pl.BlockSpec(memory_space=pltpu.VMEM)
    shape = jax.ShapeDtypeStruct(guess.shape, f32)
    scratch = [
        pltpu.VMEM((tiles, TILE, H * feats), f32),
        pltpu.VMEM((feats, H * feats), bf16),
        pltpu.VMEM((feats, H * feats), bf16),
        pltpu.VMEM((2 * cols, H * feats), bf16),
        pltpu.VMEM((APPS, Z, rows, feats), f32),
        pltpu.VMEM((APPS, H, Z, C, rows, feats), f32),
        pltpu.VMEM((APPS, tiles, C, Z, rows, TILE), f32),
        pltpu.VMEM((APPS, tiles, C, Z, rows, TILE), f32),
        pltpu.VMEM((APPS, tiles, Z, rows, TILE), f32),
        pltpu.VMEM((APPS, tiles, Z, rows, TILE), f32),
        pltpu.VMEM((2 * ITERS, T, rows, 128), f32),
        pltpu.VMEM((rows, feats), f32),
        pltpu.VMEM((rows, feats), f32),
        dma((tiles,)),
        dma((APPS, 2, Z)), dma((APPS, Z)),
        dma((APPS, Z, C)), dma((APPS, Z, C)),
        dma((APPS, Z, C, H)), dma((APPS, Z, C, H)),
        dma((APPS, tiles, C)), dma((APPS, tiles, C)),
        dma((APPS, tiles, Z)), dma((APPS, tiles, Z)),
        dma((2 * ITERS, T)), dma((2 * ITERS, T)),
    ]
    return pl.pallas_call(
        functools.partial(kernel, Z, T, C),
        out_shape=(shape, shape),
        in_specs=[pl.BlockSpec(memory_space=pl.ANY), vmem, vmem],
        out_specs=(vmem, vmem),
        scratch_shapes=scratch,
        cost_estimate=pl.CostEstimate(
            flops=APPS * 6 * cols * feats * H * feats,
            bytes_accessed=gram.size * 4,
            transcendentals=0),
        compiler_params=pltpu.CompilerParams(
            collective_id=0, has_side_effects=True, vmem_limit_bytes=56 * 1024 * 1024),
    )(gram, rhs, guess)


def general_shards(gram, rhs, guess):
    gram_tile = gram[0]
    block_cols = gram_tile.shape[1]

    def apply_total(vector):
        columns = lax.all_gather(vector, ("mp", "tcol"), axis=0, tiled=True)
        gathered = lax.all_gather(columns, "trow", axis=1, tiled=True)
        block = lax.dynamic_slice_in_dim(
            gathered, lax.axis_index("tcol") * block_cols, block_cols, 1)
        terms = lax.dot_general(block, gram_tile, NT, precision=lax.Precision.HIGHEST,
                                preferred_element_type=jnp.float32)
        return lax.psum_scatter(terms, ("mp", "tcol"), scatter_dimension=0, tiled=True)

    def squares(values):
        return lax.psum(jnp.sum(values * values, axis=1), "trow")

    merged = guess
    residual = rhs - apply_total(guess)
    direction = residual
    norm_now = squares(residual)
    for step in range(ITERS):
        image = apply_total(direction)
        curve = lax.psum(jnp.sum(direction * image, axis=1), "trow")
        alpha = norm_now / curve
        merged = merged + alpha[:, None] * direction
        residual = residual - alpha[:, None] * image
        if step + 1 < ITERS:
            norm_next = squares(residual)
            direction = residual + (norm_next / norm_now)[:, None] * direction
            norm_now = norm_next
    return (merged, residual)


def solution(mesh):
    Z, T, C = mesh.shape["mp"], mesh.shape["trow"], mesh.shape["tcol"]

    def shards(gram, rhs, guess):
        rows, feats = guess.shape
        fits = T % C == 0 and Z & (Z - 1) == 0 and rows % 16 == 0 and feats % TILE == 0
        fits = fits and Z * C * rows * feats <= 256 * 1024 and gram.shape[0] == 1
        if fits:
            return kernel_shards(Z, T, C, gram, rhs, guess)
        return general_shards(gram, rhs, guess)

    in_specs = (P("mp", "trow", "tcol"), P(("mp", "tcol"), "trow"), P(("mp", "tcol"), "trow"))
    out_specs = (P(("mp", "tcol"), "trow"), P(("mp", "tcol"), "trow"))
    return jax.shard_map(shards, mesh=mesh, in_specs=in_specs, out_specs=out_specs, check_vma=False)
```
